32 devices in a mesh: groups: 2 (over x), seq: 8 (over z, y), mp: 2 (over core).
Axes of the slice: x: 2, y: 2, z: 4, core: 2. Of those that a mesh axis runs over, the one named last changes fastest.
Arguments:
- hidden: bfloat16 [4, 2048, 512], P('groups', 'seq'), parts along dimension 0, may hold values from -6 to 6
- in_weight: bfloat16 [512, 2304], replicated, may hold values from -0.25 to 0.25
- dt_weight: bfloat16 [512, 16], replicated, may hold values from -0.25 to 0.25
- conv_weight: float32 [2, 4, 1280], replicated, may hold values from -3 to 3
- dt_bias: float32 [2, 16], replicated, may hold values from -2 to 1
- decay_rate: float32 [2, 16], replicated, may hold values from 9.765625e-06 to 0.05
- skip_gain: float32 [2, 16], replicated, may hold values from 0.5 to 1.5
- norm_gain: float32 [2, 1024], replicated, may hold values from 0.5 to 1.5
- out_weight: bfloat16 [1024, 512], replicated, may hold values from -0.1875 to 0.1875
Outputs:
- strands_out: bfloat16 [4, 2048, 1024], P('groups', 'seq', 'mp'), parts along dimension 0
The draws below stay inside these ranges and needn't reach their ends.
There are 2 independent parts, one for each index of `groups`. The reference program is written for one: setup_inputs(seed, part) draws one part's arguments, and reference() takes and returns one part's arrays. A program takes and returns all parts, laid end to end along the dimension named above; an argument that names none is the same for every part. Nothing has to cross between parts.
All inputs are finite; a program needn't handle non-finite values.
Results may differ from the reference program's by a relative error of at most 0.0051.
Values may be sent and summed in bfloat16 or wider, within the bound.
A program may use at most 256 MiB of HBM per device.

```python
import math
import jax
import jax.numpy as jnp
from jax import lax

D = 512
HEADS = 16
HEAD_DIM = 64
STATE = 128
SPAN = 256
CONV = 4
SEQS = 2
INNER = 1024
LENGTH = 2048


def levels(own_key, dims, split, least, top_value):
    loudness, own = 1.0, jax.random.fold_in(own_key, 6)
    for dim, blocks in split:
        draws = jnp.exp(jax.random.uniform(jax.random.fold_in(own, dim), (blocks,), jnp.float32, least / len(split), top_value / len(split)))
        loudness = loudness * jnp.repeat(draws, dims[dim] // blocks).reshape([-1 if axis == dim else 1 for axis in range(len(dims))])
    return loudness


def bell_draw(rng, extent, width, reach, cuts=(), dtype=jnp.bfloat16):
    drawn = width * jax.random.normal(rng, extent, jnp.float32)
    if cuts:
        drawn = drawn * levels(rng, extent, cuts, -0.22, 0.18)
    return jnp.clip(drawn, -reach, reach).astype(dtype)


def setup_inputs(seed: int = 0, part: int = 0) -> dict:
    splits = jax.random.split(jax.random.key(seed), 10)
    part_splits = jax.random.split(jax.random.fold_in(splits[9], part), 10)
    hidden = bell_draw(part_splits[0], (SEQS, LENGTH, D), 1.0, 6.0, ((1, 8),))
    in_weight = bell_draw(splits[1], (D, 2 * INNER + 2 * STATE), D ** -0.5, 0.25)
    dt_weight = bell_draw(splits[2], (D, HEADS), D ** -0.5, 0.25)
    conv_weight = bell_draw(splits[3], (2, CONV, INNER + 2 * STATE), CONV ** -0.5, 3.0, (), jnp.float32)
    dt_bias = jnp.clip(jax.random.uniform(splits[4], (2, HEADS), jnp.float32, -2.0, 1.0), -2.0, 1.0)
    decay_rate = jnp.clip(jnp.exp(jax.random.uniform(splits[5], (2, HEADS), jnp.float32, math.log(9.765624781721272e-06), math.log(0.05))), 9.765624781721272e-06, 0.05)
    skip_gain = jnp.clip(jax.random.uniform(splits[6], (2, HEADS), jnp.float32, 0.5, 1.5), 0.5, 1.5)
    norm_gain = jnp.clip(1.0 + 0.1 * jax.random.normal(splits[7], (2, INNER), jnp.float32), 0.5, 1.5)
    out_weight = bell_draw(splits[8], (INNER, D), INNER ** -0.5, 0.1875)
    return dict(hidden=hidden, in_weight=in_weight, dt_weight=dt_weight, conv_weight=conv_weight, dt_bias=dt_bias, decay_rate=decay_rate, skip_gain=skip_gain, norm_gain=norm_gain, out_weight=out_weight)


epsilon = 1e-05

def span_scan(x_rows, b_rows, c_rows, dt_rows, log_rows, initial):
    block_count = x_rows.shape[0] // SPAN
    head_count = dt_rows.shape[1]
    head_width = x_rows.shape[1] // head_count
    causal = jnp.arange(SPAN)[:, None] >= jnp.arange(SPAN)[None, :]

    def advance(carried, pieces):
        x_part, b_part, c_part, dt_part, log_part = pieces
        running = jnp.cumsum(log_part, axis=0)
        scores = jnp.dot(c_part, b_part.T, preferred_element_type=jnp.float32)
        spread = running.T[:, :, None] - running.T[:, None, :]
        mixing = jnp.where(causal, scores[None] * jnp.exp(jnp.where(causal, spread, 0.0)) * dt_part.T[:, None, :], 0.0).astype(jnp.bfloat16)
        heads_x = x_part.reshape(SPAN, head_count, head_width)
        within = jnp.einsum('hts,shp->thp', mixing.astype(jnp.float32), heads_x.astype(jnp.float32))
        across = jnp.exp(running)[:, :, None] * jnp.einsum('tn,hpn->thp', c_part.astype(jnp.float32), carried, precision=lax.Precision.HIGHEST)
        remain = jnp.exp(running[-1][None, :] - running) * dt_part
        weighted = (b_part.astype(jnp.float32)[:, None, :] * remain[:, :, None]).astype(jnp.bfloat16)
        contrib = jnp.einsum('shn,shp->hpn', weighted.astype(jnp.float32), heads_x.astype(jnp.float32))
        carried = jnp.exp(running[-1])[:, None, None] * carried + contrib
        return (carried, (within + across).reshape(SPAN, head_count * head_width))
    pieces = tuple((member.reshape(block_count, SPAN, member.shape[1]) for member in (x_rows, b_rows, c_rows, dt_rows, log_rows)))
    final_state, outputs = lax.scan(advance, initial, pieces)
    return (outputs.reshape(block_count * SPAN, head_count * head_width), final_state)

def mix_strand(inputs, in_weight, dt_weight, conv_weight, dt_bias, decay_rate, skip_gain, norm_gain, out_weight):
    length = inputs.shape[0]
    projected = jnp.dot(inputs, in_weight, preferred_element_type=jnp.float32)
    gating = projected[:, :INNER]
    mixed_in = projected[:, INNER:].astype(jnp.bfloat16)
    dt_raw = jnp.dot(inputs, dt_weight, preferred_element_type=jnp.float32)
    silu_gate = jax.nn.silu(gating)
    summed = jnp.zeros((length, INNER), jnp.float32)
    empty_state = jnp.zeros((HEADS, HEAD_DIM, STATE), jnp.float32)
    for direction in range(2):
        ordered = mixed_in if direction == 0 else mixed_in[::-1]
        padded = jnp.concatenate([jnp.zeros((CONV - 1, ordered.shape[1]), jnp.bfloat16), ordered], axis=0)
        source = padded.astype(jnp.float32)
        convolved = conv_weight[direction, 0] * source[0:length]
        for offset in range(1, CONV):
            convolved = convolved + conv_weight[direction, offset] * source[offset:offset + length]
        activated = jax.nn.silu(convolved).astype(jnp.bfloat16)
        x_rows = activated[:, :INNER]
        b_rows = activated[:, INNER:INNER + STATE]
        c_rows = activated[:, INNER + STATE:]
        dt_source = dt_raw if direction == 0 else dt_raw[::-1]
        dt_step = jax.nn.softplus(dt_source + dt_bias[direction])
        log_decay = -dt_step * decay_rate[direction]
        result_rows, final_state = span_scan(x_rows, b_rows, c_rows, dt_step, log_decay, empty_state)
        result_rows = result_rows + jnp.repeat(skip_gain[direction], HEAD_DIM)[None, :] * x_rows.astype(jnp.float32)
        if direction == 1:
            result_rows = result_rows[::-1]
        gated = result_rows * silu_gate
        gated = gated * lax.rsqrt(lax.optimization_barrier(jnp.mean(gated * gated, axis=-1, keepdims=True)) + epsilon) * norm_gain[direction]
        summed = summed + gated
    return jnp.dot(summed.astype(jnp.bfloat16), out_weight, preferred_element_type=jnp.float32).astype(jnp.bfloat16)

def reference(hidden, in_weight, dt_weight, conv_weight, dt_bias, decay_rate, skip_gain, norm_gain, out_weight):
    results = []
    for sequence in range(SEQS):
        forward_in = hidden[sequence]
        reverse_in = hidden[sequence][::-1]
        forward_out = mix_strand(forward_in, in_weight, dt_weight, conv_weight, dt_bias, decay_rate, skip_gain, norm_gain, out_weight)
        reverse_out = mix_strand(reverse_in, in_weight, dt_weight, conv_weight, dt_bias, decay_rate, skip_gain, norm_gain, out_weight)
        results.append(jnp.concatenate([forward_out, reverse_out[::-1]], axis=-1))
    return jnp.stack(results)
```

```python
import functools

import jax
import jax.numpy as jnp
from jax import lax
from jax.experimental import pallas as pl
from jax.experimental.pallas import tpu as pltpu
from jax.sharding import PartitionSpec as P

HEADS = 16
HEAD_DIM = 64
STATE = 128
CONV = 4
INNER = 1024
MIXED = INNER + 2 * STATE
ROWS = 256
CHUNKS = 4
CHUNK_HEADS = HEADS // CHUNKS
WIDTH = INNER // CHUNKS
HALO = 16
epsilon = 1e-05

F32 = jnp.float32
BF16 = jnp.bfloat16
MESH = pl.DeviceIdType.MESH
HIGHEST = lax.Precision.HIGHEST


def silu(value):
    return value / (1.0 + jnp.exp(-value))


def dot(a, b, dims=((1,), (0,)), precision=None):
    return lax.dot_general(a, b, (dims, ((), ())), preferred_element_type=F32, precision=precision)


def column(row):
    eye = lax.broadcasted_iota(jnp.int32, (HEADS, HEADS), 0) == lax.broadcasted_iota(
        jnp.int32, (HEADS, HEADS), 1
    )
    return jnp.sum(jnp.where(eye, jnp.broadcast_to(row, (HEADS, HEADS)), 0.0), axis=1, keepdims=True)


def halves(value):
    high = value.astype(BF16).astype(F32)
    return high, (value - high).astype(BF16).astype(F32)


def kernel(
    count,
    seqs,
    hidden,
    in_weight,
    dt_weight,
    conv_weight,
    dt_bias,
    decay_rate,
    skip_gain,
    norm_gain,
    out_weight,
    out,
    ext,
    act,
    local,
    gate,
    state,
    scores,
    head_rows,
    cum_cols,
    factors,
    spread_to,
    skip,
    halo,
    came,
    gone,
    halo_send,
    halo_recv,
    send_sem,
    recv_sem,
):
    me = lax.axis_index("seq")
    strand = lax.axis_index("mp")
    before, after = me > 0, me < count - 1
    has_source = (before, after)
    has_target = (after, before)
    target = (me + 1, me - 1)
    which = (strand, 1 - strand)

    barrier = pltpu.get_barrier_semaphore()

    @pl.when(before)
    def _():
        pl.semaphore_signal(barrier, inc=1, device_id={"seq": me - 1}, device_id_type=MESH)

    @pl.when(after)
    def _():
        pl.semaphore_signal(barrier, inc=1, device_id={"seq": me + 1}, device_id_type=MESH)

    inside = before & after

    @pl.when(inside)
    def _():
        pl.semaphore_wait(barrier, 2)

    @pl.when(jnp.logical_not(inside))
    def _():
        pl.semaphore_wait(barrier, 1)

    def halo_copy(d):
        first = ROWS - HALO if d == 0 else 0
        return pltpu.make_async_remote_copy(
            src_ref=hidden.at[:, pl.ds(first, HALO), :],
            dst_ref=halo.at[d],
            send_sem=halo_send.at[d],
            recv_sem=halo_recv.at[d],
            device_id={"seq": target[d]},
            device_id_type=MESH,
        )

    def chain_copy(d, i):
        return pltpu.make_async_remote_copy(
            src_ref=gone.at[d, i],
            dst_ref=came.at[d, i],
            send_sem=send_sem.at[d, i],
            recv_sem=recv_sem.at[d, i],
            device_id={"seq": target[d]},
            device_id_type=MESH,
        )

    for d in range(2):

        @pl.when(has_target[d])
        def _():
            halo_copy(d).start()

        @pl.when(jnp.logical_not(has_source[d]))
        def _():
            halo[d] = jnp.zeros(halo.shape[1:], BF16)
            came[d] = jnp.zeros(came.shape[1:], BF16)

    group_row = lax.broadcasted_iota(jnp.int32, (128, INNER), 0)
    lane_head = lax.broadcasted_iota(jnp.int32, (128, INNER), 1) // HEAD_DIM
    for kind in range(4):
        pick = (group_row == lane_head + 2 * kind * HEADS) | (
            group_row == lane_head + (2 * kind + 1) * HEADS
        )
        spread_to[kind] = jnp.where(pick, 1.0, 0.0).astype(BF16)
    head_pick = jnp.where(
        lax.broadcasted_iota(jnp.int32, (HEADS, INNER), 0)
        == lax.broadcasted_iota(jnp.int32, (HEADS, INNER), 1) // HEAD_DIM,
        1.0,
        0.0,
    )
    for d in range(2):
        row = jnp.broadcast_to(skip_gain[pl.ds(which[d], 1), :], (8, HEADS))
        skip[d] = dot(row, head_pick, precision=HIGHEST)

    row_id = lax.broadcasted_iota(jnp.int32, (ROWS, ROWS), 0)
    col_id = lax.broadcasted_iota(jnp.int32, (ROWS, ROWS), 1)

    def project(b, carry):
        mixed = dot(hidden[b], in_weight[:, INNER:])
        ext[b, pl.ds(8, ROWS), :] = mixed.astype(BF16).astype(F32)
        raw = dot(dt_weight[...], hidden[b], ((0,), (1,)))
        groups, cums = [], []
        for d in range(2):
            biased = raw + column(dt_bias[pl.ds(which[d], 1), :])
            step = jnp.maximum(biased, 0.0) + jnp.log1p(jnp.exp(-jnp.abs(biased)))
            log_decay = -step * column(decay_rate[pl.ds(which[d], 1), :])
            order = (row_id <= col_id) if d == 0 else (row_id >= col_id)
            cum = dot(log_decay, jnp.where(order, 1.0, 0.0), precision=HIGHEST)
            total = cum[:, ROWS - 1 :] if d == 0 else cum[:, :1]
            for c in range(CHUNKS):
                mine = slice(c * CHUNK_HEADS, (c + 1) * CHUNK_HEADS)
                head_rows[b, c, d] = jnp.concatenate([cum[mine], step[mine]], axis=0)
            cums.append(cum)
            groups += [*halves(jnp.exp(cum)), *halves(jnp.exp(total - cum) * step)]
        factors[b] = jnp.transpose(jnp.concatenate(groups, axis=0)).astype(BF16)
        cums.append(jnp.zeros((128 - 2 * HEADS, ROWS), F32))
        cols = jnp.transpose(jnp.concatenate(cums, axis=0))
        for c in range(CHUNKS):
            cum_cols[b, c] = cols if c == 0 else pltpu.roll(cols, 128 - c * CHUNK_HEADS, 1)
        return carry

    lax.fori_loop(0, seqs, project, 0)

    for d in range(2):

        @pl.when(has_source[d])
        def _():
            halo_copy(d).wait_recv()

        edge = dot(halo[d].reshape(seqs * HALO, halo.shape[3]), in_weight[:, INNER:])
        edge = edge.astype(BF16).astype(F32)
        for b in range(seqs):
            if d == 0:
                ext[b, pl.ds(0, 8), :] = edge[b * HALO + HALO - 8 : b * HALO + HALO]
            else:
                ext[b, pl.ds(8 + ROWS, 8), :] = edge[b * HALO : b * HALO + 8]

    def states(b, carry):
        for d in range(2):
            taps = conv_weight[which[d]]
            for first in range(0, MIXED, STATE):
                lanes = pl.ds(first, STATE)
                total = None
                for k in range(CONV):
                    start = 8 - (CONV - 1) + k if d == 0 else 8 + (CONV - 1) - k
                    term = taps[k : k + 1, first : first + STATE] * ext[b, pl.ds(start, ROWS), lanes]
                    total = term if total is None else total + term
                act[d, b, :, lanes] = silu(total).astype(BF16)
            b_part = act[d, b, :, pl.ds(INNER, STATE)]
            c_part = act[d, b, :, pl.ds(INNER + STATE, STATE)]
            for c in range(CHUNKS):
                lanes = pl.ds(c * WIDTH, WIDTH)
                remain = dot(factors[b], spread_to[2 * d + 1, :, lanes])
                weighted = (act[d, b, :, lanes].astype(F32) * remain).astype(BF16)
                gain = dot(b_part, weighted, ((0,), (0,)))
                state[d, b * CHUNKS + c] = gain

                @pl.when(jnp.logical_not(has_source[d]) & has_target[d])
                def _():
                    gone[d, b * CHUNKS + c] = gain.astype(BF16)
                    chain_copy(d, b * CHUNKS + c).start()

            causal = (row_id >= col_id) if d == 0 else (row_id <= col_id)
            scores[d, b] = jnp.where(causal, dot(c_part, b_part, ((1,), (1,))), 0.0)
        return carry

    lax.fori_loop(0, seqs, states, 0)

    half = ROWS // 2
    low_lanes = lax.broadcasted_iota(jnp.int32, (half, 2 * HEAD_DIM), 1) < HEAD_DIM

    def chunk(i, carry):
        b, c = i // CHUNKS, i % CHUNKS
        lanes = pl.ds(pl.multiple_of(c * WIDTH, WIDTH), WIDTH)
        for d in range(2):

            @pl.when(has_source[d])
            def _():
                chain_copy(d, i).wait_recv()

            @pl.when(has_source[d] & has_target[d])
            def _():
                last = 240 if d == 0 else 0
                decay = dot(factors[b, pl.ds(last, 16), :], spread_to[2 * d, :, lanes])
                decay = decay[15:16] if d == 0 else decay[0:1]
                gone[d, i] = (decay * came[d, i].astype(F32) + state[d, i]).astype(BF16)
                chain_copy(d, i).start()

        gate[b, :, lanes] = silu(dot(hidden[b], in_weight[:, lanes]))
        cols = cum_cols[b, c]
        for d in range(2):
            entering = dot(act[d, b, :, pl.ds(INNER + STATE, STATE)], came[d, i])
            entering = entering * dot(factors[b], spread_to[2 * d, :, lanes])
            x_chunk = act[d, b, :, lanes]
            rows = head_rows[b, c, d]
            base = entering + skip[d, 0:1, lanes] * x_chunk.astype(F32)
            for pair in range(CHUNK_HEADS // 2):
                inner = slice(pair * 128, pair * 128 + 128)
                x_pair = x_chunk[:, inner]
                pair_lanes = pl.ds(pl.multiple_of(c * WIDTH + pair * 128, 128), 128)
                for block in range(2):
                    t_rows = slice(block * half, block * half + half)
                    if d == 0:
                        s_rows = slice(0, half + block * half)
                    else:
                        s_rows = slice(block * half, ROWS)
                    tile = scores[d, b, t_rows, s_rows]
                    parts = []
                    for one in range(2):
                        head = pair * 2 + one
                        cum_s = rows[head : head + 1, s_rows]
                        dt_s = rows[CHUNK_HEADS + head : CHUNK_HEADS + head + 1, s_rows]
                        lane = d * HEADS + head
                        cum_t = cols[t_rows, lane : lane + 1]
                        mixing = tile * jnp.exp(jnp.minimum(cum_t - cum_s, 0.0)) * dt_s
                        parts.append(dot(mixing.astype(BF16), x_pair[s_rows]))
                    within = jnp.where(low_lanes, parts[0], parts[1])
                    local[d, b, t_rows, pair_lanes] = within + base[t_rows, inner]

        @pl.when(c == CHUNKS - 1)
        def _():
            for first in range(0, ROWS, 64):
                rows = pl.ds(first, 64)
                silu_gate = gate[b, rows, :]
                summed = None
                for d in range(2):
                    gated = local[d, b, rows, :] * silu_gate
                    mean = jnp.mean(gated * gated, axis=-1, keepdims=True)
                    gated = gated * lax.rsqrt(mean + epsilon) * norm_gain[pl.ds(which[d], 1), :]
                    summed = gated if summed is None else summed + gated
                out[b, rows, :] = dot(summed.astype(BF16), out_weight[...]).astype(BF16)

        return carry

    lax.fori_loop(0, seqs * CHUNKS, chunk, 0)

    for d in range(2):

        @pl.when(has_target[d])
        def _():
            halo_copy(d).wait_send()

            def drain(i, carry):
                chain_copy(d, i).wait_send()
                return carry

            lax.fori_loop(0, seqs * CHUNKS, drain, 0)


def on_device(hidden, *params):
    count = lax.axis_size("seq")
    seqs, rows, width = hidden.shape
    steps = seqs * CHUNKS
    vmem = pl.BlockSpec(memory_space=pltpu.VMEM)
    return pl.pallas_call(
        functools.partial(kernel, count, seqs),
        out_shape=jax.ShapeDtypeStruct((seqs, rows, params[-1].shape[1]), BF16),
        in_specs=[vmem] * 9,
        out_specs=vmem,
        scratch_shapes=[
            pltpu.VMEM((seqs, rows + 16, MIXED), F32),
            pltpu.VMEM((2, seqs, rows, MIXED), BF16),
            pltpu.VMEM((2, seqs, rows, INNER), F32),
            pltpu.VMEM((seqs, rows, INNER), F32),
            pltpu.VMEM((2, steps, STATE, WIDTH), F32),
            pltpu.VMEM((2, seqs, rows, rows), F32),
            pltpu.VMEM((seqs, CHUNKS, 2, 2 * CHUNK_HEADS, rows), F32),
            pltpu.VMEM((seqs, CHUNKS, rows, 128), F32),
            pltpu.VMEM((seqs, rows, 128), BF16),
            pltpu.VMEM((4, 128, INNER), BF16),
            pltpu.VMEM((2, 8, INNER), F32),
            pltpu.VMEM((2, seqs, HALO, width), BF16),
            pltpu.VMEM((2, steps, STATE, WIDTH), BF16),
            pltpu.VMEM((2, steps, STATE, WIDTH), BF16),
            pltpu.SemaphoreType.DMA((2,)),
            pltpu.SemaphoreType.DMA((2,)),
            pltpu.SemaphoreType.DMA((2, steps)),
            pltpu.SemaphoreType.DMA((2, steps)),
        ],
        compiler_params=pltpu.CompilerParams(
            collective_id=0, has_side_effects=True, vmem_limit_bytes=48 * 1024 * 1024
        ),
        name="mixer",
    )(hidden, *params)


def solution(mesh):
    in_specs = (P("groups", "seq", None), P(), P(), P(), P(), P(), P(), P(), P())
    out_specs = P("groups", "seq", "mp")
    return jax.shard_map(
        on_device, mesh=mesh, in_specs=in_specs, out_specs=out_specs, check_vma=False
    )
```

```python
import functools

import jax
import jax.numpy as jnp
from jax import lax
from jax.experimental import pallas as pl
from jax.experimental.pallas import tpu as pltpu
from jax.sharding import PartitionSpec as P

HEADS = 16
HEAD_DIM = 64
STATE = 128
CONV = 4
INNER = 1024
MIXED = INNER + 2 * STATE
ROWS = 256
CHUNKS = 4
CHUNK_HEADS = HEADS // CHUNKS
WIDTH = INNER // CHUNKS
HALO = 16
epsilon = 1e-05

F32 = jnp.float32
BF16 = jnp.bfloat16
MESH = pl.DeviceIdType.MESH
HIGHEST = lax.Precision.HIGHEST


def silu(value):
    return value / (1.0 + jnp.exp(-value))


def dot(a, b, dims=((1,), (0,)), precision=None):
    return lax.dot_general(a, b, (dims, ((), ())), preferred_element_type=F32, precision=precision)


def column(row):
    eye = lax.broadcasted_iota(jnp.int32, (HEADS, HEADS), 0) == lax.broadcasted_iota(
        jnp.int32, (HEADS, HEADS), 1
    )
    return jnp.sum(jnp.where(eye, jnp.broadcast_to(row, (HEADS, HEADS)), 0.0), axis=1, keepdims=True)


def halves(value):
    high = value.astype(BF16).astype(F32)
    return high, (value - high).astype(BF16).astype(F32)


def kernel(
    count,
    seqs,
    hidden,
    in_weight,
    dt_weight,
    conv_weight,
    dt_bias,
    decay_rate,
    skip_gain,
    norm_gain,
    out_weight,
    out,
    ext,
    act,
    local,
    gate,
    state,
    scores,
    head_rows,
    cum_cols,
    factors,
    spread_to,
    skip,
    halo,
    came,
    gone,
    halo_send,
    halo_recv,
    send_sem,
    recv_sem,
):
    me = lax.axis_index("seq")
    strand = lax.axis_index("mp")
    before, after = me > 0, me < count - 1
    has_source = (before, after)
    has_target = (after, before)
    target = (me + 1, me - 1)
    which = (strand, 1 - strand)

    barrier = pltpu.get_barrier_semaphore()

    @pl.when(before)
    def _():
        pl.semaphore_signal(barrier, inc=1, device_id={"seq": me - 1}, device_id_type=MESH)

    @pl.when(after)
    def _():
        pl.semaphore_signal(barrier, inc=1, device_id={"seq": me + 1}, device_id_type=MESH)

    inside = before & after

    @pl.when(inside)
    def _():
        pl.semaphore_wait(barrier, 2)

    @pl.when(jnp.logical_not(inside))
    def _():
        pl.semaphore_wait(barrier, 1)

    def halo_copy(d):
        first = ROWS - HALO if d == 0 else 0
        return pltpu.make_async_remote_copy(
            src_ref=hidden.at[:, pl.ds(first, HALO), :],
            dst_ref=halo.at[d],
            send_sem=halo_send.at[d],
            recv_sem=halo_recv.at[d],
            device_id={"seq": target[d]},
            device_id_type=MESH,
        )

    def chain_copy(d, i):
        return pltpu.make_async_remote_copy(
            src_ref=gone.at[d, i],
            dst_ref=came.at[d, i],
            send_sem=send_sem.at[d, i],
            recv_sem=recv_sem.at[d, i],
            device_id={"seq": target[d]},
            device_id_type=MESH,
        )

    for d in range(2):

        @pl.when(has_target[d])
        def _():
            halo_copy(d).start()

        @pl.when(jnp.logical_not(has_source[d]))
        def _():
            halo[d] = jnp.zeros(halo.shape[1:], BF16)
            came[d] = jnp.zeros(came.shape[1:], BF16)

    group_row = lax.broadcasted_iota(jnp.int32, (128, INNER), 0)
    lane_head = lax.broadcasted_iota(jnp.int32, (128, INNER), 1) // HEAD_DIM
    for kind in range(4):
        pick = (group_row == lane_head + 2 * kind * HEADS) | (
            group_row == lane_head + (2 * kind + 1) * HEADS
        )
        spread_to[kind] = jnp.where(pick, 1.0, 0.0).astype(BF16)
    head_pick = jnp.where(
        lax.broadcasted_iota(jnp.int32, (HEADS, INNER), 0)
        == lax.broadcasted_iota(jnp.int32, (HEADS, INNER), 1) // HEAD_DIM,
        1.0,
        0.0,
    )
    for d in range(2):
        row = jnp.broadcast_to(skip_gain[pl.ds(which[d], 1), :], (8, HEADS))
        skip[d] = dot(row, head_pick, precision=HIGHEST)

    row_id = lax.broadcasted_iota(jnp.int32, (ROWS, ROWS), 0)
    col_id = lax.broadcasted_iota(jnp.int32, (ROWS, ROWS), 1)

    def project(b, carry):
        mixed = dot(hidden[b], in_weight[:, INNER:])
        ext[b, pl.ds(8, ROWS), :] = mixed.astype(BF16).astype(F32)
        raw = dot(dt_weight[...], hidden[b], ((0,), (1,)))
        groups, cums = [], []
        for d in range(2):
            biased = raw + column(dt_bias[pl.ds(which[d], 1), :])
            step = jnp.maximum(biased, 0.0) + jnp.log1p(jnp.exp(-jnp.abs(biased)))
            log_decay = -step * column(decay_rate[pl.ds(which[d], 1), :])
            order = (row_id <= col_id) if d == 0 else (row_id >= col_id)
            cum = dot(log_decay, jnp.where(order, 1.0, 0.0), precision=HIGHEST)
            total = cum[:, ROWS - 1 :] if d == 0 else cum[:, :1]
            for c in range(CHUNKS):
                mine = slice(c * CHUNK_HEADS, (c + 1) * CHUNK_HEADS)
                head_rows[b, c, d] = jnp.concatenate([cum[mine], step[mine]], axis=0)
            cums.append(cum)
            groups += [*halves(jnp.exp(cum)), *halves(jnp.exp(total - cum) * step)]
        factors[b] = jnp.transpose(jnp.concatenate(groups, axis=0)).astype(BF16)
        cums.append(jnp.zeros((128 - 2 * HEADS, ROWS), F32))
        cols = jnp.transpose(jnp.concatenate(cums, axis=0))
        for c in range(CHUNKS):
            cum_cols[b, c] = cols if c == 0 else pltpu.roll(cols, 128 - c * CHUNK_HEADS, 1)
        return carry

    lax.fori_loop(0, seqs, project, 0)

    for d in range(2):

        @pl.when(has_source[d])
        def _():
            halo_copy(d).wait_recv()

        edge = dot(halo[d].reshape(seqs * HALO, halo.shape[3]), in_weight[:, INNER:])
        edge = edge.astype(BF16).astype(F32)
        for b in range(seqs):
            if d == 0:
                ext[b, pl.ds(0, 8), :] = edge[b * HALO + HALO - 8 : b * HALO + HALO]
            else:
                ext[b, pl.ds(8 + ROWS, 8), :] = edge[b * HALO : b * HALO + 8]

    def states(b, carry):
        for d in range(2):
            taps = conv_weight[which[d]]
            for first in range(0, MIXED, STATE):
                lanes = pl.ds(first, STATE)
                total = None
                for k in range(CONV):
                    start = 8 - (CONV - 1) + k if d == 0 else 8 + (CONV - 1) - k
                    term = taps[k : k + 1, first : first + STATE] * ext[b, pl.ds(start, ROWS), lanes]
                    total = term if total is None else total + term
                act[d, b, :, lanes] = silu(total).astype(BF16)
            b_part = act[d, b, :, pl.ds(INNER, STATE)]
            c_part = act[d, b, :, pl.ds(INNER + STATE, STATE)]
            for c in range(CHUNKS):
                lanes = pl.ds(c * WIDTH, WIDTH)
                remain = dot(factors[b], spread_to[2 * d + 1, :, lanes])
                weighted = (act[d, b, :, lanes].astype(F32) * remain).astype(BF16)
                gain = dot(b_part, weighted, ((0,), (0,)))
                state[d, b * CHUNKS + c] = gain

                @pl.when(jnp.logical_not(has_source[d]) & has_target[d])
                def _():
                    gone[d, b * CHUNKS + c] = gain.astype(BF16)
                    chain_copy(d, b * CHUNKS + c).start()

            causal = (row_id >= col_id) if d == 0 else (row_id <= col_id)
            scores[d, b] = jnp.where(causal, dot(c_part, b_part, ((1,), (1,))), 0.0)
        return carry

    lax.fori_loop(0, seqs, states, 0)

    half = ROWS // 2
    low_lanes = lax.broadcasted_iota(jnp.int32, (half, 2 * HEAD_DIM), 1) < HEAD_DIM

    steps = seqs * CHUNKS

    def advance(d, i):
        b, c = i // CHUNKS, i % CHUNKS
        lanes = pl.ds(pl.multiple_of(c * WIDTH, WIDTH), WIDTH)

        @pl.when(has_source[d])
        def _():
            chain_copy(d, i).wait_recv()

        @pl.when(has_source[d] & has_target[d])
        def _():
            last = ROWS - 16 if d == 0 else 0
            decay = dot(factors[b, pl.ds(last, 16), :], spread_to[2 * d, :, lanes])
            decay = decay[15:16] if d == 0 else decay[0:1]
            gone[d, i] = (decay * came[d, i].astype(F32) + state[d, i]).astype(BF16)
            chain_copy(d, i).start()

    def enter(d, i):
        b, c = i // CHUNKS, i % CHUNKS
        lanes = pl.ds(pl.multiple_of(c * WIDTH, WIDTH), WIDTH)
        entering = dot(act[d, b, :, pl.ds(INNER + STATE, STATE)], came[d, i])
        local[d, b, :, lanes] += entering * dot(factors[b], spread_to[2 * d, :, lanes])

    def inside_block(i):
        b, c = i // CHUNKS, i % CHUNKS
        lanes = pl.ds(pl.multiple_of(c * WIDTH, WIDTH), WIDTH)
        gate[b, :, lanes] = silu(dot(hidden[b], in_weight[:, lanes]))
        cols = cum_cols[b, c]
        for d in range(2):
            x_chunk = act[d, b, :, lanes]
            rows = head_rows[b, c, d]
            base = skip[d, 0:1, lanes] * x_chunk.astype(F32)
            for pair in range(CHUNK_HEADS // 2):
                inner = slice(pair * 128, pair * 128 + 128)
                x_pair = x_chunk[:, inner]
                pair_lanes = pl.ds(pl.multiple_of(c * WIDTH + pair * 128, 128), 128)
                for block in range(2):
                    t_rows = slice(block * half, block * half + half)
                    if d == 0:
                        s_rows = slice(0, half + block * half)
                    else:
                        s_rows = slice(block * half, ROWS)
                    tile = scores[d, b, t_rows, s_rows]
                    parts = []
                    for one in range(2):
                        head = pair * 2 + one
                        cum_s = rows[head : head + 1, s_rows]
                        dt_s = rows[CHUNK_HEADS + head : CHUNK_HEADS + head + 1, s_rows]
                        lane = d * HEADS + head
                        cum_t = cols[t_rows, lane : lane + 1]
                        mixing = tile * jnp.exp(jnp.minimum(cum_t - cum_s, 0.0)) * dt_s
                        parts.append(dot(mixing.astype(BF16), x_pair[s_rows]))
                    within = jnp.where(low_lanes, parts[0], parts[1])
                    local[d, b, t_rows, pair_lanes] = within + base[t_rows, inner]

    def finish(b):
        for first in range(0, ROWS, 64):
            rows = pl.ds(first, 64)
            silu_gate = gate[b, rows, :]
            summed = None
            for d in range(2):
                gated = local[d, b, rows, :] * silu_gate
                mean = jnp.mean(gated * gated, axis=-1, keepdims=True)
                gated = gated * lax.rsqrt(mean + epsilon) * norm_gain[pl.ds(which[d], 1), :]
                summed = gated if summed is None else summed + gated
            out[b, rows, :] = dot(summed.astype(BF16), out_weight[...]).astype(BF16)

    hops = (me, count - 1 - me)
    latest = jnp.maximum(hops[0], hops[1])

    def tick(t, carry):
        here = [(t >= hops[d]) & (t < hops[d] + steps) for d in range(2)]
        for d in range(2):

            @pl.when(here[d])
            def _():
                advance(d, t - hops[d])

        @pl.when(t < steps)
        def _():
            inside_block(t)

        for d in range(2):

            @pl.when(here[d])
            def _():
                enter(d, t - hops[d])

        done = t - latest + 1

        @pl.when((done > 0) & (done % CHUNKS == 0) & (done <= steps))
        def _():
            finish(done // CHUNKS - 1)

        return carry

    lax.fori_loop(0, latest + steps, tick, 0)

    for d in range(2):

        @pl.when(has_target[d])
        def _():
            halo_copy(d).wait_send()

            def drain(i, carry):
                chain_copy(d, i).wait_send()
                return carry

            lax.fori_loop(0, seqs * CHUNKS, drain, 0)


def on_device(hidden, *params):
    count = lax.axis_size("seq")
    seqs, rows, width = hidden.shape
    steps = seqs * CHUNKS
    vmem = pl.BlockSpec(memory_space=pltpu.VMEM)
    return pl.pallas_call(
        functools.partial(kernel, count, seqs),
        out_shape=jax.ShapeDtypeStruct((seqs, rows, params[-1].shape[1]), BF16),
        in_specs=[vmem] * 9,
        out_specs=vmem,
        scratch_shapes=[
            pltpu.VMEM((seqs, rows + 16, MIXED), F32),
            pltpu.VMEM((2, seqs, rows, MIXED), BF16),
            pltpu.VMEM((2, seqs, rows, INNER), F32),
            pltpu.VMEM((seqs, rows, INNER), F32),
            pltpu.VMEM((2, steps, STATE, WIDTH), F32),
            pltpu.VMEM((2, seqs, rows, rows), F32),
            pltpu.VMEM((seqs, CHUNKS, 2, 2 * CHUNK_HEADS, rows), F32),
            pltpu.VMEM((seqs, CHUNKS, rows, 128), F32),
            pltpu.VMEM((seqs, rows, 128), BF16),
            pltpu.VMEM((4, 128, INNER), BF16),
            pltpu.VMEM((2, 8, INNER), F32),
            pltpu.VMEM((2, seqs, HALO, width), BF16),
            pltpu.VMEM((2, steps, STATE, WIDTH), BF16),
            pltpu.VMEM((2, steps, STATE, WIDTH), BF16),
            pltpu.SemaphoreType.DMA((2,)),
            pltpu.SemaphoreType.DMA((2,)),
            pltpu.SemaphoreType.DMA((2, steps)),
            pltpu.SemaphoreType.DMA((2, steps)),
        ],
        compiler_params=pltpu.CompilerParams(
            collective_id=0, has_side_effects=True, vmem_limit_bytes=48 * 1024 * 1024
        ),
        name="mixer",
    )(hidden, *params)


def solution(mesh):
    in_specs = (P("groups", "seq", None), P(), P(), P(), P(), P(), P(), P(), P())
    out_specs = P("groups", "seq", "mp")
    return jax.shard_map(
        on_device, mesh=mesh, in_specs=in_specs, out_specs=out_specs, check_vma=False
    )
```

```python
import functools

import jax
import jax.numpy as jnp
from jax import lax
from jax.experimental import pallas as pl
from jax.experimental.pallas import tpu as pltpu
from jax.sharding import PartitionSpec as P

HEADS = 16
HEAD_DIM = 64
STATE = 128
CONV = 4
INNER = 1024
MIXED = INNER + 2 * STATE
ROWS = 256
CHUNKS = 2
CHUNK_HEADS = HEADS // CHUNKS
WIDTH = INNER // CHUNKS
HALO = 16
epsilon = 1e-05

F32 = jnp.float32
BF16 = jnp.bfloat16
MESH = pl.DeviceIdType.MESH
HIGHEST = lax.Precision.HIGHEST


def silu(value):
    half = 0.5 * value
    return half + half * jnp.tanh(half)


def dot(a, b, dims=((1,), (0,)), precision=None):
    return lax.dot_general(a, b, (dims, ((), ())), preferred_element_type=F32, precision=precision)


def column(row):
    eye = lax.broadcasted_iota(jnp.int32, (HEADS, HEADS), 0) == lax.broadcasted_iota(
        jnp.int32, (HEADS, HEADS), 1
    )
    return jnp.sum(jnp.where(eye, jnp.broadcast_to(row, (HEADS, HEADS)), 0.0), axis=1, keepdims=True)


def halves(value):
    high = value.astype(BF16).astype(F32)
    return high, (value - high).astype(BF16).astype(F32)


def kernel(
    count,
    seqs,
    hidden_hbm,
    in_weight_hbm,
    dt_weight_hbm,
    conv_weight_hbm,
    dt_bias_hbm,
    decay_rate_hbm,
    skip_gain_hbm,
    norm_gain_hbm,
    out_weight_hbm,
    out,
    hidden,
    in_weight,
    dt_weight,
    conv_weight,
    dt_bias,
    decay_rate,
    skip_gain,
    norm_gain,
    out_weight,
    ext,
    act,
    local,
    gate,
    state,
    scores,
    head_rows,
    cum_cols,
    factors,
    spread_to,
    skip,
    halo,
    pair_out,
    pair_in,
    inbox,
    came,
    gone,
    halo_send,
    halo_recv,
    pair_send,
    pair_recv,
    send_sem,
    recv_sem,
    load_sem,
):
    loads = [
        pltpu.make_async_copy(source, kept, load_sem.at[at])
        for at, (source, kept) in enumerate(
            [
                (hidden_hbm, hidden),
                (dt_weight_hbm, dt_weight),
                (in_weight_hbm.at[:, pl.ds(INNER, MIXED)], in_weight.at[:, pl.ds(INNER, MIXED)]),
                (dt_bias_hbm, dt_bias),
                (decay_rate_hbm, decay_rate),
                (skip_gain_hbm, skip_gain),
                (conv_weight_hbm, conv_weight),
                (norm_gain_hbm, norm_gain),
                (in_weight_hbm.at[:, pl.ds(0, INNER)], in_weight.at[:, pl.ds(0, INNER)]),
                (out_weight_hbm, out_weight),
            ]
        )
    ]
    for load in loads:
        load.start()
    me = lax.axis_index("seq")
    strand = lax.axis_index("mp")
    before, after = me > 0, me < count - 1
    has_source = (before, after)
    has_target = (after, before)
    target = (me + 1, me - 1)
    which = (strand, 1 - strand)

    pairs = count // 2
    odd = me % 2
    leads = (odd == 1, odd == 0)
    rank = (me // 2, pairs - 1 - me // 2)
    partner = me + 1 - 2 * odd

    barrier = pltpu.get_barrier_semaphore()
    for offset in (-2, -1, 1, 2):

        @pl.when((me + offset >= 0) & (me + offset < count))
        def _():
            pl.semaphore_signal(barrier, inc=1, device_id={"seq": me + offset}, device_id_type=MESH)

    pl.semaphore_wait(barrier, jnp.minimum(me, 2) + jnp.minimum(count - 1 - me, 2))

    def halo_copy(d):
        first = ROWS - HALO if d == 0 else 0
        return pltpu.make_async_remote_copy(
            src_ref=hidden_hbm.at[:, pl.ds(first, HALO), :],
            dst_ref=halo.at[d],
            send_sem=halo_send.at[d],
            recv_sem=halo_recv.at[d],
            device_id={"seq": target[d]},
            device_id_type=MESH,
        )

    def pair_copy(i):
        return pltpu.make_async_remote_copy(
            src_ref=pair_out.at[i],
            dst_ref=pair_in.at[i],
            send_sem=pair_send.at[i],
            recv_sem=pair_recv.at[i],
            device_id={"seq": partner},
            device_id_type=MESH,
        )

    def lead_copy(d, i):
        return pltpu.make_async_remote_copy(
            src_ref=gone.at[i],
            dst_ref=inbox.at[i],
            send_sem=send_sem.at[0, i],
            recv_sem=recv_sem.at[0, i],
            device_id={"seq": me + 2 * (1 - 2 * d)},
            device_id_type=MESH,
        )

    def share_copy(d, i):
        return pltpu.make_async_remote_copy(
            src_ref=inbox.at[i],
            dst_ref=came.at[d, i],
            send_sem=send_sem.at[1, i],
            recv_sem=recv_sem.at[1, i],
            device_id={"seq": partner},
            device_id_type=MESH,
        )

    def block_decay(d, b, lanes):
        last = ROWS - 16 if d == 0 else 0
        decay = dot(factors[b, pl.ds(last, 16), :], spread_to[2 * d, :, lanes])
        return decay[15:16] if d == 0 else decay[0:1]

    for d in range(2):

        @pl.when(has_target[d])
        def _():
            halo_copy(d).start()

        @pl.when(jnp.logical_not(has_source[d]))
        def _():
            halo[d] = jnp.zeros(halo.shape[1:], BF16)

        @pl.when((rank[d] == 0) & jnp.logical_not(leads[d]))
        def _():
            came[d] = jnp.zeros(came.shape[1:], BF16)

        @pl.when((rank[d] == 0) & leads[d])
        def _():
            inbox[...] = jnp.zeros(inbox.shape, BF16)

    group_row = lax.broadcasted_iota(jnp.int32, (128, INNER), 0)
    lane_head = lax.broadcasted_iota(jnp.int32, (128, INNER), 1) // HEAD_DIM
    for kind in range(4):
        pick = (group_row == lane_head + 2 * kind * HEADS) | (
            group_row == lane_head + (2 * kind + 1) * HEADS
        )
        spread_to[kind] = jnp.where(pick, 1.0, 0.0).astype(BF16)
    head_pick = jnp.where(
        lax.broadcasted_iota(jnp.int32, (HEADS, INNER), 0)
        == lax.broadcasted_iota(jnp.int32, (HEADS, INNER), 1) // HEAD_DIM,
        1.0,
        0.0,
    )
    for load in loads[:6]:
        load.wait()
    for d in range(2):
        row = jnp.broadcast_to(skip_gain[pl.ds(which[d], 1), :], (8, HEADS))
        skip[d] = dot(row, head_pick, precision=HIGHEST)

    row_id = lax.broadcasted_iota(jnp.int32, (ROWS, ROWS), 0)
    col_id = lax.broadcasted_iota(jnp.int32, (ROWS, ROWS), 1)

    def project(b, carry):
        mixed = dot(hidden[b], in_weight[:, INNER:])
        ext[b, pl.ds(8, ROWS), :] = mixed.astype(BF16).astype(F32)
        raw = dot(dt_weight[...], hidden[b], ((1,), (1,)))
        groups, cums = [], []
        for d in range(2):
            biased = raw + column(dt_bias[pl.ds(which[d], 1), :])
            step = jnp.maximum(biased, 0.0) + jnp.log1p(jnp.exp(-jnp.abs(biased)))
            log_decay = -step * column(decay_rate[pl.ds(which[d], 1), :])
            order = (row_id <= col_id) if d == 0 else (row_id >= col_id)
            cum = dot(log_decay, jnp.where(order, 1.0, 0.0), precision=HIGHEST)
            total = cum[:, ROWS - 1 :] if d == 0 else cum[:, :1]
            for c in range(CHUNKS):
                mine = slice(c * CHUNK_HEADS, (c + 1) * CHUNK_HEADS)
                head_rows[b, c, d] = jnp.concatenate([cum[mine], step[mine]], axis=0)
            cums.append(cum)
            groups += [*halves(jnp.exp(cum)), *halves(jnp.exp(total - cum) * step)]
        factors[b] = jnp.transpose(jnp.concatenate(groups, axis=0)).astype(BF16)
        cums.append(jnp.zeros((128 - 2 * HEADS, ROWS), F32))
        cols = jnp.transpose(jnp.concatenate(cums, axis=0))
        for c in range(CHUNKS):
            cum_cols[b, c] = cols if c == 0 else pltpu.roll(cols, 128 - c * CHUNK_HEADS, 1)
        return carry

    lax.fori_loop(0, seqs, project, 0)

    for d in range(2):

        @pl.when(has_source[d])
        def _():
            halo_copy(d).wait_recv()

        edge = dot(halo[d].reshape(seqs * HALO, halo.shape[3]), in_weight[:, INNER:])
        edge = edge.astype(BF16).astype(F32)
        for b in range(seqs):
            if d == 0:
                ext[b, pl.ds(0, 8), :] = edge[b * HALO + HALO - 8 : b * HALO + HALO]
            else:
                ext[b, pl.ds(8 + ROWS, 8), :] = edge[b * HALO : b * HALO + 8]

    def states(b, carry):
        for d in range(2):
            taps = conv_weight[which[d]]
            for first in range(0, MIXED, STATE):
                lanes = pl.ds(first, STATE)
                total = None
                for k in range(CONV):
                    start = 8 - (CONV - 1) + k if d == 0 else 8 + (CONV - 1) - k
                    term = taps[k : k + 1, first : first + STATE] * ext[b, pl.ds(start, ROWS), lanes]
                    total = term if total is None else total + term
                act[d, b, :, lanes] = silu(total).astype(BF16)
            b_part = act[d, b, :, pl.ds(INNER, STATE)]
            b_turned = jnp.transpose(b_part)
            c_part = act[d, b, :, pl.ds(INNER + STATE, STATE)]
            for c in range(CHUNKS):
                lanes = pl.ds(c * WIDTH, WIDTH)
                remain = dot(factors[b], spread_to[2 * d + 1, :, lanes])
                weighted = (act[d, b, :, lanes].astype(F32) * remain).astype(BF16)
                gain = dot(b_turned, weighted)
                state[d, b * CHUNKS + c] = gain

                @pl.when(jnp.logical_not(leads[d]))
                def _():
                    i = b * CHUNKS + c
                    high, low = halves(block_decay(d, b, lanes))
                    row = lax.broadcasted_iota(jnp.int32, (16, WIDTH), 0)
                    pair_out[i, pl.ds(0, STATE), :] = gain.astype(BF16)
                    pair_out[i, pl.ds(STATE, 16), :] = jnp.where(row == 0, high, low).astype(BF16)
                    pair_copy(i).start()

            causal = (row_id >= col_id) if d == 0 else (row_id <= col_id)
            scores[d, b] = jnp.where(causal, dot(c_part, b_part, ((1,), (1,))), 0.0)
        return carry

    loads[6].wait()
    lax.fori_loop(0, seqs, states, 0)
    for load in loads[7:]:
        load.wait()

    half = ROWS // 2
    low_lanes = lax.broadcasted_iota(jnp.int32, (half, 2 * HEAD_DIM), 1) < HEAD_DIM

    steps = seqs * CHUNKS

    def advance(d, i):
        b, c = i // CHUNKS, i % CHUNKS
        lanes = pl.ds(pl.multiple_of(c * WIDTH, WIDTH), WIDTH)

        @pl.when((rank[d] > 0) & jnp.logical_not(leads[d]))
        def _():
            share_copy(d, i).wait_recv()

        @pl.when(leads[d])
        def _():
            @pl.when(rank[d] > 0)
            def _():
                lead_copy(d, i).wait_recv()
                share_copy(d, i).start()

            pair_copy(i).wait_recv()
            decay = pair_in[i, pl.ds(STATE, 16), :].astype(F32)
            decay = decay[0:1] + decay[1:2]
            entry = decay * inbox[i].astype(F32) + pair_in[i, pl.ds(0, STATE), :].astype(F32)
            came[d, i] = entry.astype(BF16)

            @pl.when(rank[d] < pairs - 1)
            def _():
                gone[i] = (block_decay(d, b, lanes) * entry + state[d, i]).astype(BF16)
                lead_copy(d, i).start()

    def enter(d, i):
        b, c = i // CHUNKS, i % CHUNKS
        lanes = pl.ds(pl.multiple_of(c * WIDTH, WIDTH), WIDTH)
        entering = dot(act[d, b, :, pl.ds(INNER + STATE, STATE)], came[d, i])
        local[d, b, :, lanes] += entering * dot(factors[b], spread_to[2 * d, :, lanes])

    def inside_block(i):
        b, c = i // CHUNKS, i % CHUNKS
        lanes = pl.ds(pl.multiple_of(c * WIDTH, WIDTH), WIDTH)
        gate[b, :, lanes] = silu(dot(hidden[b], in_weight[:, lanes]))
        cols = cum_cols[b, c]
        for d in range(2):
            x_chunk = act[d, b, :, lanes]
            rows = head_rows[b, c, d]
            base = skip[d, 0:1, lanes] * x_chunk.astype(F32)
            for pair in range(CHUNK_HEADS // 2):
                inner = slice(pair * 128, pair * 128 + 128)
                x_pair = x_chunk[:, inner]
                pair_lanes = pl.ds(pl.multiple_of(c * WIDTH + pair * 128, 128), 128)
                for block in range(2):
                    t_rows = slice(block * half, block * half + half)
                    if d == 0:
                        s_rows = slice(0, half + block * half)
                    else:
                        s_rows = slice(block * half, ROWS)
                    tile = scores[d, b, t_rows, s_rows]
                    parts = []
                    for one in range(2):
                        head = pair * 2 + one
                        cum_s = rows[head : head + 1, s_rows]
                        dt_s = rows[CHUNK_HEADS + head : CHUNK_HEADS + head + 1, s_rows]
                        lane = d * HEADS + head
                        cum_t = cols[t_rows, lane : lane + 1]
                        mixing = tile * jnp.exp(jnp.minimum(cum_t - cum_s, 0.0)) * dt_s
                        parts.append(dot(mixing.astype(BF16), x_pair[s_rows]))
                    within = jnp.where(low_lanes, parts[0], parts[1])
                    local[d, b, t_rows, pair_lanes] = within + base[t_rows, inner]

    def finish(b):
        for first in range(0, ROWS, 64):
            rows = pl.ds(first, 64)
            silu_gate = gate[b, rows, :]
            summed = None
            for d in range(2):
                gated = local[d, b, rows, :] * silu_gate
                mean = jnp.mean(gated * gated, axis=-1, keepdims=True)
                gated = gated * lax.rsqrt(mean + epsilon) * norm_gain[pl.ds(which[d], 1), :]
                summed = gated if summed is None else summed + gated
            out[b, rows, :] = dot(summed.astype(BF16), out_weight[...]).astype(BF16)

    hops = (rank[0] + 1 - odd, rank[1] + odd)
    latest = jnp.maximum(hops[0], hops[1])

    def tick(t, carry):
        here = [(t >= hops[d]) & (t < hops[d] + steps) for d in range(2)]
        for d in range(2):

            @pl.when(here[d])
            def _():
                advance(d, t - hops[d])

        @pl.when(t < steps)
        def _():
            inside_block(t)

        for d in range(2):

            @pl.when(here[d])
            def _():
                enter(d, t - hops[d])

        done = t - latest + 1

        @pl.when((done > 0) & (done % CHUNKS == 0) & (done <= steps))
        def _():
            finish(done // CHUNKS - 1)

        return carry

    lax.fori_loop(0, latest + steps, tick, 0)

    for d in range(2):

        @pl.when(has_target[d])
        def _():
            halo_copy(d).wait_send()

        @pl.when(leads[d] & (rank[d] < pairs - 1))
        def _():
            def drain_lead(i, carry):
                lead_copy(d, i).wait_send()
                return carry

            lax.fori_loop(0, steps, drain_lead, 0)

        @pl.when(leads[d] & (rank[d] > 0))
        def _():
            def drain_share(i, carry):
                share_copy(d, i).wait_send()
                return carry

            lax.fori_loop(0, steps, drain_share, 0)

    def drain_pair(i, carry):
        pair_copy(i).wait_send()
        return carry

    lax.fori_loop(0, steps, drain_pair, 0)


def on_device(hidden, *params):
    count = lax.axis_size("seq")
    seqs, rows, width = hidden.shape
    steps = seqs * CHUNKS
    values = (hidden, params[0], params[1].T, *params[2:])
    vmem = pl.BlockSpec(memory_space=pltpu.VMEM)
    return pl.pallas_call(
        functools.partial(kernel, count, seqs),
        out_shape=jax.ShapeDtypeStruct((seqs, rows, params[-1].shape[1]), BF16),
        in_specs=[pl.BlockSpec(memory_space=pl.ANY)] * 9,
        out_specs=vmem,
        scratch_shapes=[
            *[pltpu.VMEM(value.shape, value.dtype) for value in values],
            pltpu.VMEM((seqs, rows + 16, MIXED), F32),
            pltpu.VMEM((2, seqs, rows, MIXED), BF16),
            pltpu.VMEM((2, seqs, rows, INNER), F32),
            pltpu.VMEM((seqs, rows, INNER), F32),
            pltpu.VMEM((2, steps, STATE, WIDTH), F32),
            pltpu.VMEM((2, seqs, rows, rows), F32),
            pltpu.VMEM((seqs, CHUNKS, 2, 2 * CHUNK_HEADS, rows), F32),
            pltpu.VMEM((seqs, CHUNKS, rows, 128), F32),
            pltpu.VMEM((seqs, rows, 128), BF16),
            pltpu.VMEM((4, 128, INNER), BF16),
            pltpu.VMEM((2, 8, INNER), F32),
            pltpu.VMEM((2, seqs, HALO, width), BF16),
            pltpu.VMEM((steps, STATE + 16, WIDTH), BF16),
            pltpu.VMEM((steps, STATE + 16, WIDTH), BF16),
            pltpu.VMEM((steps, STATE, WIDTH), BF16),
            pltpu.VMEM((2, steps, STATE, WIDTH), BF16),
            pltpu.VMEM((steps, STATE, WIDTH), BF16),
            pltpu.SemaphoreType.DMA((2,)),
            pltpu.SemaphoreType.DMA((2,)),
            pltpu.SemaphoreType.DMA((steps,)),
            pltpu.SemaphoreType.DMA((steps,)),
            pltpu.SemaphoreType.DMA((2, steps)),
            pltpu.SemaphoreType.DMA((2, steps)),
            pltpu.SemaphoreType.DMA((10,)),
        ],
        compiler_params=pltpu.CompilerParams(
            collective_id=0, has_side_effects=True, vmem_limit_bytes=48 * 1024 * 1024
        ),
        name="mixer",
    )(*values)


def solution(mesh):
    in_specs = (P("groups", "seq", None), P(), P(), P(), P(), P(), P(), P(), P())
    out_specs = P("groups", "seq", "mp")
    return jax.shard_map(
        on_device, mesh=mesh, in_specs=in_specs, out_specs=out_specs, check_vma=False
    )
```

```python
import functools

import jax
import jax.numpy as jnp
from jax import lax
from jax.experimental import pallas as pl
from jax.experimental.pallas import tpu as pltpu
from jax.sharding import PartitionSpec as P

HEADS = 16
HEAD_DIM = 64
STATE = 128
CONV = 4
INNER = 1024
MIXED = INNER + 2 * STATE
ROWS = 256
CHUNKS = 2
CHUNK_HEADS = HEADS // CHUNKS
WIDTH = INNER // CHUNKS
HALO = 16
epsilon = 1e-05

F32 = jnp.float32
BF16 = jnp.bfloat16
MESH = pl.DeviceIdType.MESH
HIGHEST = lax.Precision.HIGHEST


def silu(value):
    half = 0.5 * value
    return half + half * jnp.tanh(half)


def dot(a, b, dims=((1,), (0,)), precision=None):
    return lax.dot_general(a, b, (dims, ((), ())), preferred_element_type=F32, precision=precision)


def column(row):
    eye = lax.broadcasted_iota(jnp.int32, (HEADS, HEADS), 0) == lax.broadcasted_iota(
        jnp.int32, (HEADS, HEADS), 1
    )
    return jnp.sum(jnp.where(eye, jnp.broadcast_to(row, (HEADS, HEADS)), 0.0), axis=1, keepdims=True)


def halves(value):
    high = value.astype(BF16).astype(F32)
    return high, (value - high).astype(BF16).astype(F32)


def kernel(
    count,
    seqs,
    hidden_hbm,
    in_weight_hbm,
    dt_weight_hbm,
    conv_weight_hbm,
    dt_bias_hbm,
    decay_rate_hbm,
    skip_gain_hbm,
    norm_gain_hbm,
    out_weight_hbm,
    out,
    hidden,
    in_weight,
    dt_weight,
    conv_weight,
    dt_bias,
    decay_rate,
    skip_gain,
    norm_gain,
    out_weight,
    ext,
    act,
    local,
    gate,
    state,
    scores,
    head_rows,
    cum_cols,
    factors,
    spread_to,
    skip,
    halo,
    pair_out,
    pair_in,
    inbox,
    came,
    gone,
    halo_send,
    halo_recv,
    pair_send,
    pair_recv,
    send_sem,
    recv_sem,
    load_sem,
):
    loads = [
        pltpu.make_async_copy(source, kept, load_sem.at[at])
        for at, (source, kept) in enumerate(
            [
                (hidden_hbm, hidden),
                (dt_weight_hbm, dt_weight),
                (in_weight_hbm.at[:, pl.ds(INNER, MIXED)], in_weight.at[:, pl.ds(INNER, MIXED)]),
                (dt_bias_hbm, dt_bias),
                (decay_rate_hbm, decay_rate),
                (skip_gain_hbm, skip_gain),
                (conv_weight_hbm, conv_weight),
                (norm_gain_hbm, norm_gain),
                (in_weight_hbm.at[:, pl.ds(0, INNER)], in_weight.at[:, pl.ds(0, INNER)]),
                (out_weight_hbm, out_weight),
            ]
        )
    ]
    for load in loads:
        load.start()
    me = lax.axis_index("seq")
    strand = lax.axis_index("mp")
    before, after = me > 0, me < count - 1
    has_source = (before, after)
    has_target = (after, before)
    target = (me + 1, me - 1)
    which = (strand, 1 - strand)

    pairs = count // 2
    odd = me % 2
    leads = (odd == 1, odd == 0)
    rank = (me // 2, pairs - 1 - me // 2)
    partner = me + 1 - 2 * odd

    barrier = pltpu.get_barrier_semaphore()
    for offset in (-2, -1, 1, 2):

        @pl.when((me + offset >= 0) & (me + offset < count))
        def _():
            pl.semaphore_signal(barrier, inc=1, device_id={"seq": me + offset}, device_id_type=MESH)

    pl.semaphore_wait(barrier, jnp.minimum(me, 2) + jnp.minimum(count - 1 - me, 2))

    def halo_copy(d):
        first = ROWS - HALO if d == 0 else 0
        return pltpu.make_async_remote_copy(
            src_ref=hidden_hbm.at[:, pl.ds(first, HALO), :],
            dst_ref=halo.at[d],
            send_sem=halo_send.at[d],
            recv_sem=halo_recv.at[d],
            device_id={"seq": target[d]},
            device_id_type=MESH,
        )

    def pair_copy(i):
        return pltpu.make_async_remote_copy(
            src_ref=pair_out.at[i],
            dst_ref=pair_in.at[i],
            send_sem=pair_send.at[i],
            recv_sem=pair_recv.at[i],
            device_id={"seq": partner},
            device_id_type=MESH,
        )

    def lead_copy(d, i):
        return pltpu.make_async_remote_copy(
            src_ref=gone.at[i],
            dst_ref=inbox.at[i],
            send_sem=send_sem.at[0, i],
            recv_sem=recv_sem.at[0, i],
            device_id={"seq": me + 2 * (1 - 2 * d)},
            device_id_type=MESH,
        )

    def share_copy(d, i):
        return pltpu.make_async_remote_copy(
            src_ref=inbox.at[i],
            dst_ref=came.at[d, i],
            send_sem=send_sem.at[1, i],
            recv_sem=recv_sem.at[1, i],
            device_id={"seq": partner},
            device_id_type=MESH,
        )

    def block_decay(d, b, lanes):
        last = ROWS - 16 if d == 0 else 0
        decay = dot(factors[b, pl.ds(last, 16), :], spread_to[2 * d, :, lanes])
        return decay[15:16] if d == 0 else decay[0:1]

    for d in range(2):

        @pl.when(has_target[d])
        def _():
            halo_copy(d).start()

        @pl.when(jnp.logical_not(has_source[d]))
        def _():
            halo[d] = jnp.zeros(halo.shape[1:], BF16)

        @pl.when((rank[d] == 0) & jnp.logical_not(leads[d]))
        def _():
            came[d] = jnp.zeros(came.shape[1:], BF16)

        @pl.when((rank[d] == 0) & leads[d])
        def _():
            inbox[...] = jnp.zeros(inbox.shape, BF16)

    group_row = lax.broadcasted_iota(jnp.int32, (128, INNER), 0)
    lane_head = lax.broadcasted_iota(jnp.int32, (128, INNER), 1) // HEAD_DIM
    for kind in range(4):
        pick = (group_row == lane_head + 2 * kind * HEADS) | (
            group_row == lane_head + (2 * kind + 1) * HEADS
        )
        spread_to[kind] = jnp.where(pick, 1.0, 0.0).astype(BF16)
    head_pick = jnp.where(
        lax.broadcasted_iota(jnp.int32, (HEADS, INNER), 0)
        == lax.broadcasted_iota(jnp.int32, (HEADS, INNER), 1) // HEAD_DIM,
        1.0,
        0.0,
    )
    for load in loads[:6]:
        load.wait()
    for d in range(2):
        row = jnp.broadcast_to(skip_gain[pl.ds(which[d], 1), :], (8, HEADS))
        skip[d] = dot(row, head_pick, precision=HIGHEST)

    row_id = lax.broadcasted_iota(jnp.int32, (ROWS, ROWS), 0)
    col_id = lax.broadcasted_iota(jnp.int32, (ROWS, ROWS), 1)

    def project(b, carry):
        mixed = dot(hidden[b], in_weight[:, INNER:])
        ext[b, pl.ds(8, ROWS), :] = mixed.astype(BF16).astype(F32)
        raw = dot(dt_weight[...], hidden[b], ((1,), (1,)))
        groups, cums = [], []
        for d in range(2):
            biased = raw + column(dt_bias[pl.ds(which[d], 1), :])
            step = jnp.maximum(biased, 0.0) + jnp.log1p(jnp.exp(-jnp.abs(biased)))
            log_decay = -step * column(decay_rate[pl.ds(which[d], 1), :])
            order = (row_id <= col_id) if d == 0 else (row_id >= col_id)
            cum = dot(log_decay, jnp.where(order, 1.0, 0.0), precision=HIGHEST)
            total = cum[:, ROWS - 1 :] if d == 0 else cum[:, :1]
            for c in range(CHUNKS):
                mine = slice(c * CHUNK_HEADS, (c + 1) * CHUNK_HEADS)
                head_rows[b, c, d] = jnp.concatenate([cum[mine], step[mine]], axis=0)
            cums.append(cum)
            groups += [*halves(jnp.exp(cum)), *halves(jnp.exp(total - cum) * step)]
        factors[b] = jnp.transpose(jnp.concatenate(groups, axis=0)).astype(BF16)
        cums.append(jnp.zeros((128 - 2 * HEADS, ROWS), F32))
        cols = jnp.transpose(jnp.concatenate(cums, axis=0))
        for c in range(CHUNKS):
            cum_cols[b, c] = cols if c == 0 else pltpu.roll(cols, 128 - c * CHUNK_HEADS, 1)
        return carry

    lax.fori_loop(0, seqs, project, 0)

    for d in range(2):

        @pl.when(has_source[d])
        def _():
            halo_copy(d).wait_recv()

        edge = dot(halo[d].reshape(seqs * HALO, halo.shape[3]), in_weight[:, INNER:])
        edge = edge.astype(BF16).astype(F32)
        for b in range(seqs):
            if d == 0:
                ext[b, pl.ds(0, 8), :] = edge[b * HALO + HALO - 8 : b * HALO + HALO]
            else:
                ext[b, pl.ds(8 + ROWS, 8), :] = edge[b * HALO : b * HALO + 8]

    def states(b, carry):
        for d in range(2):
            taps = conv_weight[which[d]]
            for first in range(0, MIXED, STATE):
                lanes = pl.ds(first, STATE)
                total = None
                for k in range(CONV):
                    start = 8 - (CONV - 1) + k if d == 0 else 8 + (CONV - 1) - k
                    term = taps[k : k + 1, first : first + STATE] * ext[b, pl.ds(start, ROWS), lanes]
                    total = term if total is None else total + term
                act[d, b, :, lanes] = silu(total).astype(BF16)
            b_part = act[d, b, :, pl.ds(INNER, STATE)]
            b_turned = jnp.transpose(b_part)
            c_part = act[d, b, :, pl.ds(INNER + STATE, STATE)]
            for c in range(CHUNKS):
                lanes = pl.ds(c * WIDTH, WIDTH)
                remain = dot(factors[b], spread_to[2 * d + 1, :, lanes])
                weighted = (act[d, b, :, lanes].astype(F32) * remain).astype(BF16)
                gain = dot(b_turned, weighted)
                state[d, b * CHUNKS + c] = gain

                @pl.when(jnp.logical_not(leads[d]))
                def _():
                    i = b * CHUNKS + c
                    high, low = halves(block_decay(d, b, lanes))
                    row = lax.broadcasted_iota(jnp.int32, (16, WIDTH), 0)
                    pair_out[i, pl.ds(0, STATE), :] = gain.astype(BF16)
                    pair_out[i, pl.ds(STATE, 16), :] = jnp.where(row == 0, high, low).astype(BF16)
                    pair_copy(i).start()

            causal = (row_id >= col_id) if d == 0 else (row_id <= col_id)
            scores[d, b] = jnp.where(causal, dot(c_part, b_part, ((1,), (1,))), 0.0)
        return carry

    loads[6].wait()
    lax.fori_loop(0, seqs, states, 0)
    for load in loads[7:]:
        load.wait()

    half = ROWS // 2
    low_lanes = lax.broadcasted_iota(jnp.int32, (half, 2 * HEAD_DIM), 1) < HEAD_DIM

    steps = seqs * CHUNKS

    def advance(d, i):
        b, c = i // CHUNKS, i % CHUNKS
        lanes = pl.ds(pl.multiple_of(c * WIDTH, WIDTH), WIDTH)

        @pl.when(leads[d])
        def _():
            @pl.when(rank[d] > 0)
            def _():
                lead_copy(d, i).wait_recv()
                share_copy(d, i).start()

            pair_copy(i).wait_recv()
            decay = pair_in[i, pl.ds(STATE, 16), :].astype(F32)
            decay = decay[0:1] + decay[1:2]
            entry = decay * inbox[i].astype(F32) + pair_in[i, pl.ds(0, STATE), :].astype(F32)
            came[d, i] = entry.astype(BF16)

            @pl.when(rank[d] < pairs - 1)
            def _():
                gone[i] = (block_decay(d, b, lanes) * entry + state[d, i]).astype(BF16)
                lead_copy(d, i).start()

    def enter(d, i):
        b, c = i // CHUNKS, i % CHUNKS
        lanes = pl.ds(pl.multiple_of(c * WIDTH, WIDTH), WIDTH)
        @pl.when((rank[d] > 0) & jnp.logical_not(leads[d]))
        def _():
            share_copy(d, i).wait_recv()

        entering = dot(act[d, b, :, pl.ds(INNER + STATE, STATE)], came[d, i])
        local[d, b, :, lanes] += entering * dot(factors[b], spread_to[2 * d, :, lanes])

    def inside_block(i):
        b, c = i // CHUNKS, i % CHUNKS
        lanes = pl.ds(pl.multiple_of(c * WIDTH, WIDTH), WIDTH)
        gate[b, :, lanes] = silu(dot(hidden[b], in_weight[:, lanes]))
        cols = cum_cols[b, c]
        for d in range(2):
            x_chunk = act[d, b, :, lanes]
            rows = head_rows[b, c, d]
            base = skip[d, 0:1, lanes] * x_chunk.astype(F32)
            for pair in range(CHUNK_HEADS // 2):
                inner = slice(pair * 128, pair * 128 + 128)
                x_pair = x_chunk[:, inner]
                pair_lanes = pl.ds(pl.multiple_of(c * WIDTH + pair * 128, 128), 128)
                for block in range(2):
                    t_rows = slice(block * half, block * half + half)
                    if d == 0:
                        s_rows = slice(0, half + block * half)
                    else:
                        s_rows = slice(block * half, ROWS)
                    tile = scores[d, b, t_rows, s_rows]
                    parts = []
                    for one in range(2):
                        head = pair * 2 + one
                        cum_s = rows[head : head + 1, s_rows]
                        dt_s = rows[CHUNK_HEADS + head : CHUNK_HEADS + head + 1, s_rows]
                        lane = d * HEADS + head
                        cum_t = cols[t_rows, lane : lane + 1]
                        mixing = tile * jnp.exp(jnp.minimum(cum_t - cum_s, 0.0)) * dt_s
                        parts.append(dot(mixing.astype(BF16), x_pair[s_rows]))
                    within = jnp.where(low_lanes, parts[0], parts[1])
                    local[d, b, t_rows, pair_lanes] = within + base[t_rows, inner]

    def finish(b):
        for first in range(0, ROWS, 64):
            rows = pl.ds(first, 64)
            silu_gate = gate[b, rows, :]
            summed = None
            for d in range(2):
                gated = local[d, b, rows, :] * silu_gate
                mean = jnp.mean(gated * gated, axis=-1, keepdims=True)
                gated = gated * lax.rsqrt(mean + epsilon) * norm_gain[pl.ds(which[d], 1), :]
                summed = gated if summed is None else summed + gated
            out[b, rows, :] = dot(summed.astype(BF16), out_weight[...]).astype(BF16)

    hops = (rank[0] + 1 - odd, rank[1] + odd)
    latest = jnp.maximum(hops[0], hops[1])

    def tick(t, carry):
        here = [(t >= hops[d]) & (t < hops[d] + steps) for d in range(2)]
        for d in range(2):

            @pl.when(here[d])
            def _():
                advance(d, t - hops[d])

        @pl.when(t < steps)
        def _():
            inside_block(t)

        for d in range(2):

            @pl.when(here[d])
            def _():
                enter(d, t - hops[d])

        done = t - latest + 1

        @pl.when((done > 0) & (done % CHUNKS == 0) & (done <= steps))
        def _():
            finish(done // CHUNKS - 1)

        return carry

    lax.fori_loop(0, latest + steps, tick, 0)

    for d in range(2):

        @pl.when(has_target[d])
        def _():
            halo_copy(d).wait_send()

        @pl.when(leads[d] & (rank[d] < pairs - 1))
        def _():
            def drain_lead(i, carry):
                lead_copy(d, i).wait_send()
                return carry

            lax.fori_loop(0, steps, drain_lead, 0)

        @pl.when(leads[d] & (rank[d] > 0))
        def _():
            def drain_share(i, carry):
                share_copy(d, i).wait_send()
                return carry

            lax.fori_loop(0, steps, drain_share, 0)

    def drain_pair(i, carry):
        pair_copy(i).wait_send()
        return carry

    lax.fori_loop(0, steps, drain_pair, 0)


def on_device(hidden, *params):
    count = lax.axis_size("seq")
    seqs, rows, width = hidden.shape
    steps = seqs * CHUNKS
    values = (hidden, params[0], params[1].T, *params[2:])
    vmem = pl.BlockSpec(memory_space=pltpu.VMEM)
    return pl.pallas_call(
        functools.partial(kernel, count, seqs),
        out_shape=jax.ShapeDtypeStruct((seqs, rows, params[-1].shape[1]), BF16),
        in_specs=[pl.BlockSpec(memory_space=pl.ANY)] * 9,
        out_specs=vmem,
        scratch_shapes=[
            *[pltpu.VMEM(value.shape, value.dtype) for value in values],
            pltpu.VMEM((seqs, rows + 16, MIXED), F32),
            pltpu.VMEM((2, seqs, rows, MIXED), BF16),
            pltpu.VMEM((2, seqs, rows, INNER), F32),
            pltpu.VMEM((seqs, rows, INNER), F32),
            pltpu.VMEM((2, steps, STATE, WIDTH), F32),
            pltpu.VMEM((2, seqs, rows, rows), F32),
            pltpu.VMEM((seqs, CHUNKS, 2, 2 * CHUNK_HEADS, rows), F32),
            pltpu.VMEM((seqs, CHUNKS, rows, 128), F32),
            pltpu.VMEM((seqs, rows, 128), BF16),
            pltpu.VMEM((4, 128, INNER), BF16),
            pltpu.VMEM((2, 8, INNER), F32),
            pltpu.VMEM((2, seqs, HALO, width), BF16),
            pltpu.VMEM((steps, STATE + 16, WIDTH), BF16),
            pltpu.VMEM((steps, STATE + 16, WIDTH), BF16),
            pltpu.VMEM((steps, STATE, WIDTH), BF16),
            pltpu.VMEM((2, steps, STATE, WIDTH), BF16),
            pltpu.VMEM((steps, STATE, WIDTH), BF16),
            pltpu.SemaphoreType.DMA((2,)),
            pltpu.SemaphoreType.DMA((2,)),
            pltpu.SemaphoreType.DMA((steps,)),
            pltpu.SemaphoreType.DMA((steps,)),
            pltpu.SemaphoreType.DMA((2, steps)),
            pltpu.SemaphoreType.DMA((2, steps)),
            pltpu.SemaphoreType.DMA((10,)),
        ],
        compiler_params=pltpu.CompilerParams(
            collective_id=0, has_side_effects=True, vmem_limit_bytes=48 * 1024 * 1024
        ),
        name="mixer",
    )(*values)


def solution(mesh):
    in_specs = (P("groups", "seq", None), P(), P(), P(), P(), P(), P(), P(), P())
    out_specs = P("groups", "seq", "mp")
    return jax.shard_map(
        on_device, mesh=mesh, in_specs=in_specs, out_specs=out_specs, check_vma=False
    )
```
